256 devices in a mesh: ab: 64 (over z, y_hi, x), cd: 4 (over y_lo, core).
Axes of the slice: x: 4, y: 4 (y_hi: 2, y_lo: 2; y = y_hi * 2 + y_lo), z: 8, core: 2. Of those that a mesh axis runs over, the one named last changes fastest.
Arguments:
- amplitudes: bfloat16 [6144, 8192], P(('cd', 'ab')), may hold values from -6 to 6
- integrals: bfloat16 [8192, 8192], P('ab', 'cd'), may hold values from -0.1875 to 0.1875
- ab_symmetry: int32 [8192], P('ab'), may hold values from 0 to 7, as said below
- cd_symmetry: int32 [8192], replicated, may hold values from 0 to 7, as said below
- ij_symmetry: int32 [6144], P('cd'), may hold values from 0 to 7, as said below
Outputs:
- ladder: bfloat16 [6144, 8192], P('cd', 'ab')
The draws below stay inside these ranges and needn't reach their ends.
Inputs may be any that keep to these rules, and one draw needn't show every extreme that they name: `ab_symmetry`: irrep labels of the eight irreps of D2h. `cd_symmetry`: irrep labels of the eight irreps of D2h. `ij_symmetry`: irrep labels of the eight irreps of D2h.
All inputs are finite; a program needn't handle non-finite values.
Results may differ from the reference program's by a relative error of at most 0.001.
Values may be sent and summed in bfloat16 or wider, within the bound.
No kernel may reach another device: no remote copies, remote signals or barrier semaphores. Data moves between devices by JAX's collectives and lax.ppermute only.
A program may use at most 128 MiB of HBM per device.

```python
import jax
import jax.numpy as jnp
from jax import lax

AB = 8192
CD = 8192
PAIRS = 6144


def shared_irrep(key):
    return jax.random.randint(key, (), 0, 8, dtype=jnp.int32)


def irrep_labels(key, length, dominant):
    region_key, heavy_key, pick_key = jax.random.split(key, 3)
    place = jnp.arange(length, dtype=jnp.int32)
    region = place * 16 // length
    offset = jax.random.randint(region_key, (), 0, 4, dtype=jnp.int32)
    single = (region + offset) % 4 == 0
    heavy = jax.random.randint(heavy_key, (length,), 0, 10, dtype=jnp.int32) < 6
    other = jax.random.randint(pick_key, (length,), 0, 8, dtype=jnp.int32)
    return jnp.where(single | heavy, dominant, other).astype(jnp.int32)


def draw_ab_symmetry(key, part):
    dominant = shared_irrep(key)
    key = jax.random.fold_in(key, 11)
    return irrep_labels(key, AB, dominant)


def draw_cd_symmetry(key, part):
    dominant = shared_irrep(key)
    key = jax.random.fold_in(key, 23)
    return irrep_labels(key, CD, dominant)


def draw_ij_symmetry(key, part):
    dominant = shared_irrep(key)
    key = jax.random.fold_in(key, 37)
    return irrep_labels(key, PAIRS, dominant)


def levels(key, extent, cuts, least, largest):
    factor_of, own = 1.0, jax.random.fold_in(key, 6)
    for dim, parts in cuts:
        draws = jnp.exp(jax.random.uniform(jax.random.fold_in(own, dim), (parts,), jnp.float32, least / len(cuts), largest / len(cuts)))
        factor_of = factor_of * jnp.repeat(draws, extent[dim] // parts).reshape([-1 if axis == dim else 1 for axis in range(len(extent))])
    return factor_of


def normal_values(rng, shape, scale, limit, shards=(), held_as=jnp.bfloat16):
    drawn = scale * jax.random.normal(rng, shape, jnp.float32)
    if shards:
        drawn = drawn * levels(rng, shape, shards, -0.22, 0.18)
    return jnp.clip(drawn, -limit, limit).astype(held_as)


def setup_inputs(seed: int = 0) -> dict:
    arg_keys = jax.random.split(jax.random.key(seed), 6)
    return {
        "amplitudes": normal_values(arg_keys[0], (PAIRS, CD), 1.0, 6.0, ((0, 256),)),
        "integrals": normal_values(arg_keys[1], (AB, CD), (CD // 8) ** -0.5, 0.1875, ((0, 64), (1, 4))),
        "ab_symmetry": draw_ab_symmetry(jax.random.fold_in(arg_keys[5], 71), 0),
        "cd_symmetry": draw_cd_symmetry(jax.random.fold_in(arg_keys[5], 71), 0),
        "ij_symmetry": draw_ij_symmetry(jax.random.fold_in(arg_keys[5], 71), 0),
    }


def reference(amplitudes, integrals, ab_symmetry, cd_symmetry, ij_symmetry):
    allowed = ab_symmetry[:, None] == cd_symmetry[None, :]
    masked_integrals = jnp.where(allowed, integrals, jnp.zeros_like(integrals))
    contracted = lax.dot_general(amplitudes, masked_integrals, (((1,), (1,)), ((), ())), preferred_element_type=jnp.float32)
    keep = ij_symmetry[:, None] == ab_symmetry[None, :]
    return jnp.where(keep, contracted, jnp.zeros_like(contracted)).astype(jnp.bfloat16)
```

```python
import jax
import jax.numpy as jnp
from jax import lax
from jax.sharding import Mesh, PartitionSpec as P

AXES = ("z", "h", "x", "l", "k")
SIZES = (8, 2, 4, 2, 2)


def shift(value, axis, step, size):
    return lax.ppermute(value, axis, [(i, (i + step) % size) for i in range(size)])


def ring_of_four(block):
    below = shift(block, "x", 1, 4)
    above = shift(block, "x", 3, 4)
    half = block.shape[0] // 2
    far = jnp.concatenate(
        [shift(below[:half], "x", 1, 4), shift(above[half:], "x", 3, 4)], axis=0
    )
    return [block, below, far, above]


def local(amplitudes, integrals, ab_symmetry, cd_symmetry, ij_symmetry):
    rows, cols = amplitudes.shape
    width = integrals.shape[1]
    z, h, x = lax.axis_index("z"), lax.axis_index("h"), lax.axis_index("x")
    mine = (z * 2 + h) * 4 + x
    slab_labels = lax.dynamic_slice_in_dim(ij_symmetry, mine * rows, rows)
    allowed = slab_labels[:, None] == cd_symmetry[None, :]
    masked = jnp.where(allowed, amplitudes, jnp.zeros_like(amplitudes))

    other = shift(integrals, "h", 1, 2)
    blocks = ring_of_four(integrals) + ring_of_four(other)
    gathered = jnp.concatenate(blocks, axis=0)

    split = jnp.swapaxes(masked.reshape(rows, 4, width), 0, 1)
    swapped = lax.all_to_all(split, ("l", "k"), split_axis=0, concat_axis=0, tiled=True)
    lines = lax.all_gather(swapped.reshape(4 * rows, width), "z", axis=0, tiled=True)

    partial = lax.dot_general(
        lines, gathered, (((1,), (1,)), ((), ())), preferred_element_type=jnp.float32
    )
    partial = partial.reshape(8, 2, 2, rows, 8 * 128)
    k, l = lax.axis_index("k"), lax.axis_index("l")

    def reduce_over(value, axis, index):
        keep = lax.dynamic_index_in_dim(value, index, 1, keepdims=False)
        give = lax.dynamic_index_in_dim(value, 1 - index, 1, keepdims=False)
        return keep + shift(give, axis, 1, 2)

    summed = reduce_over(partial.swapaxes(1, 2), "k", k)
    summed = reduce_over(summed, "l", l)
    summed = summed.astype(jnp.bfloat16).reshape(8, rows, 2, 4, 128)
    home = []
    for dh in range(2):
        for dx in range(4):
            part = summed[:, :, dh, dx]
            if dh or dx:
                pairs = [
                    (a * 4 + b, ((a + dh) % 2) * 4 + (b - dx) % 4)
                    for a in range(2)
                    for b in range(4)
                ]
                part = lax.ppermute(part, ("h", "x"), pairs)
            home.append(part)
    home = jnp.stack(home).reshape(2, 4, 8, rows, 128)
    home = jnp.roll(home, (h, x), axis=(0, 1))
    out = home.transpose(2, 0, 1, 3, 4).reshape(64 * rows, 128)
    keep = ij_symmetry[:, None] == ab_symmetry[None, :]
    return jnp.where(keep, out, jnp.zeros_like(out))


def solution(mesh):
    fine = Mesh(mesh.devices.reshape(SIZES), AXES)
    ab, cd = ("z", "h", "x"), ("l", "k")
    placed = (P(cd + ab, None), P(ab, cd), P(ab), P(), P(cd))
    return jax.shard_map(
        local, mesh=fine, in_specs=placed, out_specs=P(cd, ab), check_vma=False
    )
```

```python
import jax
import jax.numpy as jnp
from jax import lax
from jax.sharding import Mesh, PartitionSpec as P

AXES = ("z", "h", "x", "l", "k")
SIZES = {"z": 8, "h": 2, "x": 4, "l": 2, "k": 2}
ARRIVAL = (0, -1, 1, -2, 2, -3, 3, 4)


def shift(value, axis, step):
    size = SIZES[axis]
    return lax.ppermute(value, axis, [(i, (i + step) % size) for i in range(size)])


def after(values, others):
    return lax.optimization_barrier((tuple(values), tuple(others)))[0]


def far_of(below, above):
    half = below.shape[0] // 2
    return [shift(below[:half], "x", 1), shift(above[half:], "x", -1)]


def product(lines, gathered):
    return lax.dot_general(
        lines, gathered, (((1,), (1,)), ((), ())), preferred_element_type=jnp.float32
    )


def local(amplitudes, integrals, ab_symmetry, cd_symmetry, ij_symmetry):
    rows = amplitudes.shape[0]
    width = integrals.shape[1]
    at = {name: lax.axis_index(name) for name in AXES}
    l, k = at["l"], at["k"]

    first = ((at["z"] * 2 + at["h"]) * 4 + at["x"]) * rows
    slab_labels = lax.dynamic_slice_in_dim(ij_symmetry, first, rows)

    def columns(l, k):
        start = (l * 2 + k) * width
        labels = lax.dynamic_slice_in_dim(cd_symmetry, start, width)
        part = lax.dynamic_slice_in_dim(amplitudes, start, width, axis=1)
        return jnp.where(slab_labels[:, None] == labels[None, :], part, jnp.zeros_like(part))

    far = shift(jnp.concatenate([columns(1 - l, k), columns(1 - l, 1 - k)], axis=0), "l", 1)
    give = jnp.concatenate([columns(l, 1 - k), far[rows:]], axis=0)
    slabs = jnp.concatenate([columns(l, k), far[:rows], shift(give, "k", 1)], axis=0)

    half = 2 * rows
    up, down = [slabs], [slabs]
    for _ in range(3):
        up.append(shift(up[-1], "z", 1))
        down.append(shift(down[-1], "z", -1))
    opposite = [shift(up[-1][:half], "z", 1), shift(down[-1][half:], "z", -1)]

    below, above = shift(integrals, "x", 1), shift(integrals, "x", -1)
    (block,) = after((integrals,), (below, above))
    other = shift(block, "h", 1)
    middle = far_of(below, above)
    gathered = [integrals, below, *middle, above]
    (other,) = after((other,), middle)
    below, above = shift(other, "x", 1), shift(other, "x", -1)
    gathered += [other, below, *far_of(below, above), above]
    gathered = jnp.concatenate(gathered, axis=0)

    def core_sum(parts):
        n = len(parts)
        own = jnp.concatenate([p[:half] for p in parts], axis=0)
        got = shift(product(jnp.concatenate([p[half:] for p in parts], axis=0), gathered), "k", 1)
        return (product(own, gathered) + got).reshape(n, 2, rows, 8 * 128)

    def packed(summed):
        give = summed.reshape(-1, summed.shape[-1])
        top = jnp.maximum(jnp.max(jnp.abs(give), axis=0, keepdims=True), 1e-30)
        power = jnp.floor(jnp.log2(32768.0 / top))
        give = (give * jnp.exp2(power)).astype(jnp.float16)
        power = jnp.broadcast_to(power, (8, power.shape[1])).astype(jnp.float16)
        return jnp.concatenate([give, power], axis=0)

    def unpacked(got):
        n = got.shape[0] - 8
        got = got.astype(jnp.float32)
        return got[:n] * jnp.exp2(-got[n : n + 1])

    def gives(summed):
        near, other = summed[..., : 4 * 128], summed[..., 4 * 128 :]
        return packed(near[:, 1]), packed(other[:, 0]), packed(other[:, 1])

    flip = [(0, 3), (1, 2), (2, 1), (3, 0)]

    def exchanged(summed, given, in_turn):
        got_l = shift(given[0], "l", 1)
        others = after(given[1:], (got_l,)) if in_turn else given[1:]
        got_h, got_hl = shift(others[0], "h", 1), lax.ppermute(others[1], ("h", "l"), flip)
        own = summed[:, 0, :, : 4 * 128].reshape(-1, 4 * 128) + unpacked(got_l)
        return jnp.stack([own, unpacked(got_h) + unpacked(got_hl)]).astype(jnp.bfloat16)

    early = core_sum([slabs, up[1], down[1], up[2], down[2], up[3], down[3]])
    early_give = gives(early)
    opposite = after(opposite, early_give)
    early = exchanged(early, early_give, True)
    both = product(jnp.concatenate(opposite, axis=0), gathered)
    late = (both[:half] + shift(both[half:], "k", 1)).reshape(1, 2, rows, 8 * 128)
    late = exchanged(late, gives(late), False)
    result = jnp.concatenate([early, late], axis=1)
    home = [result[:, :, :128]]
    home += [shift(result[:, :, dx * 128 : dx * 128 + 128], "x", -dx) for dx in (1, 2, 3)]
    out = jnp.stack(home).reshape(4, 2, 8, rows, 128)
    order = [ARRIVAL.index(d if d < 5 else d - 8) for d in range(8)]
    out = out[:, :, jnp.array(order)].transpose(2, 1, 0, 3, 4)
    out = jnp.roll(out, (at["z"], at["h"], at["x"]), axis=(0, 1, 2)).reshape(64 * rows, 128)
    keep = ij_symmetry[:, None] == ab_symmetry[None, :]
    return jnp.where(keep, out, jnp.zeros_like(out))


def solution(mesh):
    fine = Mesh(mesh.devices.reshape(tuple(SIZES.values())), AXES)
    ab, cd = ("z", "h", "x"), ("l", "k")
    placed = (P(cd + ab, None), P(ab, cd), P(ab), P(), P(cd))
    return jax.shard_map(
        local, mesh=fine, in_specs=placed, out_specs=P(cd, ab), check_vma=False
    )
```

```python
import jax
import jax.numpy as jnp
from jax import lax
from jax.sharding import Mesh, PartitionSpec as P

AXES = ("z", "h", "x", "l", "k")
SIZES = {"z": 8, "h": 2, "x": 4, "l": 2, "k": 2}
ARRIVAL = (0, -1, 1, -2, 2, -3, 3, 4)


def shift(value, axis, step):
    size = SIZES[axis]
    return lax.ppermute(value, axis, [(i, (i + step) % size) for i in range(size)])


def after(values, others):
    return lax.optimization_barrier((tuple(values), tuple(others)))[0]


def far_of(below, above):
    half = below.shape[0] // 2
    return [shift(below[:half], "x", 1), shift(above[half:], "x", -1)]


def local(amplitudes, integrals, ab_symmetry, cd_symmetry, ij_symmetry):
    rows = amplitudes.shape[0]
    width = integrals.shape[1]
    at = {name: lax.axis_index(name) for name in AXES}
    l, k = at["l"], at["k"]

    first = ((at["z"] * 2 + at["h"]) * 4 + at["x"]) * rows
    slab_labels = lax.dynamic_slice_in_dim(ij_symmetry, first, rows)

    def columns(l, k):
        start = (l * 2 + k) * width
        labels = lax.dynamic_slice_in_dim(cd_symmetry, start, width)
        part = lax.dynamic_slice_in_dim(amplitudes, start, width, axis=1)
        return jnp.where(slab_labels[:, None] == labels[None, :], part, jnp.zeros_like(part))

    def chip_columns(l):
        return jnp.concatenate([columns(l, k), columns(l, 1 - k)], axis=1)

    far = shift(chip_columns(1 - l), "l", 1)
    slabs = jnp.concatenate([chip_columns(l), far], axis=0)

    up, down = [slabs], [slabs]
    for _ in range(3):
        up.append(shift(up[-1], "z", 1))
        down.append(shift(down[-1], "z", -1))
    opposite = lax.optimization_barrier([shift(up[-1][:rows], "z", 1), shift(down[-1][rows:], "z", -1)])
    lines = jnp.concatenate([slabs, up[1], down[1], up[2], down[2], up[3], down[3], *opposite], axis=0)

    below, above = shift(integrals, "x", 1), shift(integrals, "x", -1)
    (block,) = after((integrals,), (below, above))
    other = shift(block, "h", 1)
    middle = far_of(below, above)
    near = jnp.concatenate([integrals, below, *middle, above], axis=0)
    near_there = shift(near, "k", 1)
    (other,) = after((other,), middle)
    below, above = shift(other, "x", 1), shift(other, "x", -1)
    sides = jnp.concatenate([other, below, above], axis=0)
    sides_there = shift(sides, "k", 1)
    middle = jnp.concatenate(far_of(*after((below, above), (near_there,))), axis=0)
    (middle,) = after((middle,), (sides_there,))
    middle_there = shift(middle, "k", 1)

    def product(here, there):
        both = (here, lines[:, :width]), (there, lines[:, width:])
        parts = [
            lax.dot_general(line, block, (((1,), (1,)), ((), ())), preferred_element_type=jnp.float32)
            for block, line in both
        ]
        return (parts[0] + parts[1]).reshape(8, 2, rows, 4 * 128)

    def in_order(sides, middle):
        return jnp.concatenate([sides[:256], middle, sides[256:]], axis=0)

    near = product(near, near_there)
    other = product(in_order(sides, middle), in_order(sides_there, middle_there))

    def packed(summed):
        give = summed.reshape(-1, summed.shape[-1])
        step = jnp.maximum(jnp.max(jnp.abs(give), axis=0, keepdims=True), 1e-30) * (1 / 32512.0)
        power = jnp.ceil(jnp.log2(step) * 128.0)
        give = jnp.round(give * jnp.exp2(power * (-1 / 128.0))).astype(jnp.int16)
        power = jnp.broadcast_to(power, (8, power.shape[1])).astype(jnp.int16)
        return jnp.concatenate([give, power], axis=0)

    def unpacked(got):
        n = got.shape[0] - 8
        got = got.astype(jnp.float32)
        return got[:n] * jnp.exp2(got[n : n + 1] * (1 / 128.0))

    got_l = shift(packed(near[:, 1]), "l", 1)
    got_h = shift(packed(other[:, 0]), "h", 1)
    got_hl = lax.ppermute(packed(other[:, 1]), ("h", "l"), [(0, 3), (1, 2), (2, 1), (3, 0)])
    own = near[:, 0].reshape(-1, 4 * 128) + unpacked(got_l)
    result = jnp.stack([own, unpacked(got_h) + unpacked(got_hl)]).astype(jnp.bfloat16)
    home = [result[:, :, :128]]
    home += [shift(result[:, :, dx * 128 : dx * 128 + 128], "x", -dx) for dx in (1, 2, 3)]
    out = jnp.stack(home).reshape(4, 2, 8, rows, 128)
    order = [ARRIVAL.index(d if d < 5 else d - 8) for d in range(8)]
    out = out[:, :, jnp.array(order)].transpose(2, 1, 0, 3, 4)
    out = jnp.roll(out, (at["z"], at["h"], at["x"]), axis=(0, 1, 2)).reshape(64 * rows, 128)
    keep = ij_symmetry[:, None] == ab_symmetry[None, :]
    return jnp.where(keep, out, jnp.zeros_like(out))


def solution(mesh):
    fine = Mesh(mesh.devices.reshape(tuple(SIZES.values())), AXES)
    ab, cd = ("z", "h", "x"), ("l", "k")
    placed = (P(cd + ab, None), P(ab, cd), P(ab), P(), P(cd))
    return jax.shard_map(
        local, mesh=fine, in_specs=placed, out_specs=P(cd, ab), check_vma=False
    )
```

```python
import jax
import jax.numpy as jnp
from jax import lax
from jax.sharding import Mesh, PartitionSpec as P

AXES = ("z", "h", "x", "l", "k")
SIZES = {"z": 8, "h": 2, "x": 4, "l": 2, "k": 2}
ARRIVAL = (0, -1, 1, -2, 2, -3, 3, 4)


def shift(value, axis, step):
    size = SIZES[axis]
    return lax.ppermute(value, axis, [(i, (i + step) % size) for i in range(size)])


def after(values, others):
    return lax.optimization_barrier((tuple(values), tuple(others)))[0]


def far_of(below, above):
    half = below.shape[0] // 2
    return [shift(below[:half], "x", 1), shift(above[half:], "x", -1)]


def local(amplitudes, integrals, ab_symmetry, cd_symmetry, ij_symmetry):
    rows = amplitudes.shape[0]
    width = integrals.shape[1]
    at = {name: lax.axis_index(name) for name in AXES}
    l, k = at["l"], at["k"]

    first = ((at["z"] * 2 + at["h"]) * 4 + at["x"]) * rows
    slab_labels = lax.dynamic_slice_in_dim(ij_symmetry, first, rows)

    def columns(l, k):
        start = (l * 2 + k) * width
        labels = lax.dynamic_slice_in_dim(cd_symmetry, start, width)
        part = lax.dynamic_slice_in_dim(amplitudes, start, width, axis=1)
        return jnp.where(slab_labels[:, None] == labels[None, :], part, jnp.zeros_like(part))

    def chip_columns(l):
        return jnp.concatenate([columns(l, k), columns(l, 1 - k)], axis=1)

    give = chip_columns(1 - l)
    far = shift(give, "l", 1)
    slabs = jnp.concatenate([chip_columns(l), far], axis=0)

    up, down = [slabs], [slabs]
    for _ in range(3):
        up.append(shift(up[-1], "z", 1))
        down.append(shift(down[-1], "z", -1))
    opposite = lax.optimization_barrier([shift(up[-1][:rows], "z", 1), shift(down[-1][rows:], "z", -1)])
    lines = jnp.concatenate([slabs, up[1], down[1], up[2], down[2], up[3], down[3], *opposite], axis=0)

    (block,) = after((integrals,), (give,))
    below, above = shift(block, "x", 1), shift(block, "x", -1)
    (block,) = after((integrals,), (far,))
    other = shift(block, "h", 1)
    middle = far_of(below, above)
    middle = jnp.concatenate(middle, axis=0)
    near = jnp.concatenate([integrals, below, middle, above], axis=0)
    near_there = shift(near, "k", 1)
    (other,) = after((other,), (middle,))
    middle = shift(middle, "h", 1)
    below, above = shift(other, "x", 1), shift(other, "x", -1)
    sides = jnp.concatenate([other, below, above], axis=0)
    sides_there = shift(sides, "k", 1)
    middle_there = shift(middle, "k", 1)

    def product(lines, here, there):
        both = (here, lines[:, :width]), (there, lines[:, width:])
        parts = [
            lax.dot_general(line, block, (((1,), (1,)), ((), ())), preferred_element_type=jnp.float32)
            for block, line in both
        ]
        return (parts[0] + parts[1]).reshape(8, 2, rows, 4 * 128)

    def in_order(sides, middle):
        return jnp.concatenate([sides[:256], middle, sides[256:]], axis=0)

    other = product(lines, in_order(sides, middle), in_order(sides_there, middle_there))

    def packed(summed):
        give = summed.reshape(-1, summed.shape[-1])
        step = jnp.maximum(jnp.max(jnp.abs(give), axis=0, keepdims=True), 1e-30) * (1 / 32512.0)
        power = jnp.ceil(jnp.log2(step) * 128.0)
        give = jnp.round(give * jnp.exp2(power * (-1 / 128.0))).astype(jnp.int16)
        power = jnp.broadcast_to(power, (8, power.shape[1])).astype(jnp.int16)
        return jnp.concatenate([give, power], axis=0)

    def unpacked(got):
        n = got.shape[0] - 8
        got = got.astype(jnp.float32)
        return got[:n] * jnp.exp2(got[n : n + 1] * (1 / 128.0))

    to_h, to_hl = packed(other[:, 0]), packed(other[:, 1])
    near = product(after((lines,), (to_h, to_hl))[0], near, near_there)
    got_l = shift(packed(near[:, 1]), "l", 1)
    got_h = shift(to_h, "h", 1)
    got_hl = lax.ppermute(to_hl, ("h", "l"), [(0, 3), (1, 2), (2, 1), (3, 0)])
    own = near[:, 0].reshape(-1, 4 * 128) + unpacked(got_l)
    result = jnp.stack([own, unpacked(got_h) + unpacked(got_hl)]).astype(jnp.bfloat16)
    home = [result[:, :, :128]]
    home += [shift(result[:, :, dx * 128 : dx * 128 + 128], "x", -dx) for dx in (1, 2, 3)]
    out = jnp.stack(home).reshape(4, 2, 8, rows, 128)
    order = [ARRIVAL.index(d if d < 5 else d - 8) for d in range(8)]
    out = out[:, :, jnp.array(order)].transpose(2, 1, 0, 3, 4)
    out = jnp.roll(out, (at["z"], at["h"], at["x"]), axis=(0, 1, 2)).reshape(64 * rows, 128)
    keep = ij_symmetry[:, None] == ab_symmetry[None, :]
    return jnp.where(keep, out, jnp.zeros_like(out))


def solution(mesh):
    fine = Mesh(mesh.devices.reshape(tuple(SIZES.values())), AXES)
    ab, cd = ("z", "h", "x"), ("l", "k")
    placed = (P(cd + ab, None), P(ab, cd), P(ab), P(), P(cd))
    return jax.shard_map(
        local, mesh=fine, in_specs=placed, out_specs=P(cd, ab), check_vma=False
    )
```

```python
import jax
import jax.numpy as jnp
from jax import lax
from jax.sharding import Mesh, PartitionSpec as P

AXES = ("z", "h", "x", "l", "k")
SIZES = {"z": 8, "h": 2, "x": 4, "l": 2, "k": 2}


def shift(value, axis, step):
    size = SIZES[axis]
    return lax.ppermute(value, axis, [(i, (i + step) % size) for i in range(size)])


def after(values, others):
    return lax.optimization_barrier((tuple(values), tuple(others)))[0]


def far_of(below, above):
    half = below.shape[0] // 2
    return [shift(below[:half], "x", 1), shift(above[half:], "x", -1)]


def local(amplitudes, integrals, ab_symmetry, cd_symmetry, ij_symmetry):
    rows = amplitudes.shape[0]
    width = integrals.shape[1]
    at = {name: lax.axis_index(name) for name in AXES}
    l, k = at["l"], at["k"]

    first = ((at["z"] * 2 + at["h"]) * 4 + at["x"]) * rows
    slab_labels = lax.dynamic_slice_in_dim(ij_symmetry, first, rows)

    def columns(l, k):
        start = (l * 2 + k) * width
        labels = lax.dynamic_slice_in_dim(cd_symmetry, start, width)
        part = lax.dynamic_slice_in_dim(amplitudes, start, width, axis=1)
        return jnp.where(slab_labels[:, None] == labels[None, :], part, jnp.zeros_like(part))

    def chip_columns(l):
        return jnp.concatenate([columns(l, k), columns(l, 1 - k)], axis=1)

    give = chip_columns(1 - l)
    far = shift(give, "l", 1)
    mine = chip_columns(l)
    slabs = jnp.concatenate([mine, far], axis=0)

    up, down = [slabs], [slabs]
    for _ in range(3):
        up.append(shift(up[-1], "z", 1))
        down.append(shift(down[-1], "z", -1))
    opposite = [shift(up[-1][:rows], "z", 1), shift(down[-1][rows:], "z", -1)]
    opposite = lax.optimization_barrier(opposite)
    lines = jnp.zeros((8, 2 * rows, 2 * width), amplitudes.dtype)
    blocks = [slabs, up[1], down[1], up[2], down[2], up[3], down[3], jnp.concatenate(opposite, axis=0)]
    for step, block in zip((0, -1, 1, -2, 2, -3, 3, 4), blocks):
        lines = lax.dynamic_update_index_in_dim(lines, block, (at["z"] + step) % 8, 0)
    lines = lines.reshape(16 * rows, 2 * width)

    masked = integrals
    (block,) = after((masked,), (give,))
    below, above = shift(block, "x", 1), shift(block, "x", -1)
    (block,) = after((masked,), (far,))
    other = shift(block, "h", 1)
    middle = jnp.concatenate(far_of(below, above), axis=0)
    near = jnp.concatenate([masked, below, middle, above], axis=0)
    (other,) = after((other,), (middle,))
    middle = shift(middle, "h", 1)
    below, above = shift(other, "x", 1), shift(other, "x", -1)
    sides = jnp.concatenate([other, below, above], axis=0)
    near_there = shift(near, "k", 1)
    sides_there = shift(sides, "k", 1)
    middle_there = shift(middle, "k", 1)

    def product(lines, here, there):
        both = (here, lines[:, :width]), (there, lines[:, width:])
        parts = [
            lax.dot_general(line, block, (((1,), (1,)), ((), ())), preferred_element_type=jnp.float32)
            for block, line in both
        ]
        return (parts[0] + parts[1]).reshape(8, 2, rows, 4 * 128)

    def in_order(sides, middle):
        return jnp.concatenate([sides[:256], middle, sides[256:]], axis=0)

    other = product(lines, in_order(sides, middle), in_order(sides_there, middle_there))

    def packed(summed):
        give = summed.reshape(-1, summed.shape[-1])
        step = jnp.maximum(jnp.max(jnp.abs(give), axis=0, keepdims=True), 1e-30) * (1 / 32512.0)
        power = jnp.ceil(jnp.log2(step) * 128.0)
        give = jnp.round(give * jnp.exp2(power * (-1 / 128.0))).astype(jnp.int16)
        power = jnp.broadcast_to(power, (8, power.shape[1])).astype(jnp.int16)
        return jnp.concatenate([give, power], axis=0)

    def unpacked(got):
        n = got.shape[0] - 8
        got = got.astype(jnp.float32)
        return got[:n] * jnp.exp2(got[n : n + 1] * (1 / 128.0))

    to_h, to_hl = packed(other[:, 0]), packed(other[:, 1])
    near = product(after((lines,), (to_hl,))[0], near, near_there)
    got_l = shift(packed(near[:, 1]), "l", 1)
    got_h = shift(to_h, "h", 1)
    got_hl = lax.ppermute(to_hl, ("h", "l"), [(0, 3), (1, 2), (2, 1), (3, 0)])
    own = near[:, 0].reshape(-1, 4 * 128) + unpacked(got_l)
    other = unpacked(got_h) + unpacked(got_hl)
    result = jnp.stack([own, other]).astype(jnp.bfloat16)
    home = [result[:, :, :128]]
    home += [shift(result[:, :, dx * 128 : dx * 128 + 128], "x", -dx) for dx in (1, 2, 3)]

    out = jnp.stack(home).reshape(4, 2, 8, rows, 128)
    out = out.transpose(2, 1, 0, 3, 4)
    out = jnp.roll(out, (at["h"], at["x"],), axis=(1, 2,)).reshape(64 * rows, 128)
    keep = ij_symmetry[:, None] == ab_symmetry[None, :]
    return jnp.where(keep, out, jnp.zeros_like(out))


def solution(mesh):
    fine = Mesh(mesh.devices.reshape(tuple(SIZES.values())), AXES)
    ab, cd = ("z", "h", "x"), ("l", "k")
    placed = (P(cd + ab, None), P(ab, cd), P(ab), P(), P(cd))
    return jax.shard_map(
        local, mesh=fine, in_specs=placed, out_specs=P(cd, ab), check_vma=False
    )
```

```python
import jax
import jax.numpy as jnp
from jax import lax
from jax.sharding import Mesh, PartitionSpec as P

AXES = ("z", "h", "x", "l", "k")
SIZES = {"z": 8, "h": 2, "x": 4, "l": 2, "k": 2}


def shift(value, axis, step):
    size = SIZES[axis]
    return lax.ppermute(value, axis, [(i, (i + step) % size) for i in range(size)])


def after(values, others):
    return lax.optimization_barrier((tuple(values), tuple(others)))[0]


def far_of(below, above):
    half = below.shape[0] // 2
    return [shift(below[:half], "x", 1), shift(above[half:], "x", -1)]


def local(amplitudes, integrals, ab_symmetry, cd_symmetry, ij_symmetry):
    rows = amplitudes.shape[0]
    width = integrals.shape[1]
    at = {name: lax.axis_index(name) for name in AXES}
    l, k = at["l"], at["k"]

    first = ((at["z"] * 2 + at["h"]) * 4 + at["x"]) * rows
    slab_labels = lax.dynamic_slice_in_dim(ij_symmetry, first, rows)

    def columns(l, k):
        start = (l * 2 + k) * width
        labels = lax.dynamic_slice_in_dim(cd_symmetry, start, width)
        part = lax.dynamic_slice_in_dim(amplitudes, start, width, axis=1)
        return jnp.where(slab_labels[:, None] == labels[None, :], part, jnp.zeros_like(part))

    def chip_columns(l):
        return jnp.concatenate([columns(l, k), columns(l, 1 - k)], axis=1)

    give = chip_columns(1 - l)
    far = shift(give, "l", 1)
    mine = chip_columns(l)
    slabs = jnp.concatenate([mine, far], axis=0)

    up, down = [slabs], [slabs]
    for _ in range(3):
        up.append(shift(up[-1], "z", 1))
        down.append(shift(down[-1], "z", -1))
    opposite = [shift(up[-1][:rows], "z", 1), shift(down[-1][rows:], "z", -1)]
    opposite = lax.optimization_barrier(opposite)
    lines = jnp.zeros((8, 2 * rows, 2 * width), amplitudes.dtype)
    blocks = [slabs, up[1], down[1], up[2], down[2], up[3], down[3], jnp.concatenate(opposite, axis=0)]
    for step, block in zip((0, -1, 1, -2, 2, -3, 3, 4), blocks):
        lines = lax.dynamic_update_index_in_dim(lines, block, (at["z"] + step) % 8, 0)
    lines = lines.reshape(16 * rows, 2 * width)

    masked = integrals
    (block,) = after((masked,), (give,))
    below, above = shift(block, "x", 1), shift(block, "x", -1)
    (block,) = after((masked,), (far,))
    other = shift(block, "h", 1)
    middle = jnp.concatenate(far_of(below, above), axis=0)
    near = jnp.concatenate([masked, below, middle, above], axis=0)
    middle = shift(middle, "h", 1)
    below, above = shift(other, "x", 1), shift(other, "x", -1)
    sides = jnp.concatenate([other, below, above], axis=0)
    near_there = shift(near, "k", 1)
    sides_there = shift(sides, "k", 1)
    middle_there = shift(middle, "k", 1)

    def product(lines, here, there):
        both = (here, lines[:, :width]), (there, lines[:, width:])
        parts = [
            lax.dot_general(line, block, (((1,), (1,)), ((), ())), preferred_element_type=jnp.float32)
            for block, line in both
        ]
        return (parts[0] + parts[1]).reshape(8, 2, rows, 4 * 128)

    def in_order(sides, middle):
        return jnp.concatenate([sides[:256], middle, sides[256:]], axis=0)

    other = product(lines, in_order(sides, middle), in_order(sides_there, middle_there))

    def packed(summed):
        give = summed.reshape(-1, summed.shape[-1])
        step = jnp.maximum(jnp.max(jnp.abs(give), axis=0, keepdims=True), 1e-30) * (1 / 32512.0)
        power = jnp.ceil(jnp.log2(step) * 128.0)
        give = jnp.round(give * jnp.exp2(power * (-1 / 128.0))).astype(jnp.int16)
        power = jnp.broadcast_to(power, (8, power.shape[1])).astype(jnp.int16)
        return jnp.concatenate([give, power], axis=0)

    def unpacked(got):
        n = got.shape[0] - 8
        got = got.astype(jnp.float32)
        return got[:n] * jnp.exp2(got[n : n + 1] * (1 / 128.0))

    to_h, to_hl = packed(other[:, 0]), packed(other[:, 1])
    near = product(after((lines,), (to_hl,))[0], near, near_there)
    got_l = shift(packed(near[:, 1]), "l", 1)
    got_h = shift(to_h, "h", 1)
    got_hl = lax.ppermute(to_hl, ("h", "l"), [(0, 3), (1, 2), (2, 1), (3, 0)])
    own = near[:, 0].reshape(-1, 4 * 128) + unpacked(got_l)
    other = unpacked(got_h) + unpacked(got_hl)
    result = jnp.stack([own, other]).astype(jnp.bfloat16)
    home = [result[:, :, :128]]
    home += [shift(result[:, :, dx * 128 : dx * 128 + 128], "x", -dx) for dx in (1, 2, 3)]

    out = jnp.stack(home).reshape(4, 2, 8, rows, 128)
    out = out.transpose(2, 1, 0, 3, 4)
    out = jnp.roll(out, (at["h"], at["x"],), axis=(1, 2,)).reshape(64 * rows, 128)
    keep = ij_symmetry[:, None] == ab_symmetry[None, :]
    return jnp.where(keep, out, jnp.zeros_like(out))


def solution(mesh):
    fine = Mesh(mesh.devices.reshape(tuple(SIZES.values())), AXES)
    ab, cd = ("z", "h", "x"), ("l", "k")
    placed = (P(cd + ab, None), P(ab, cd), P(ab), P(), P(cd))
    return jax.shard_map(
        local, mesh=fine, in_specs=placed, out_specs=P(cd, ab), check_vma=False
    )
```

```python
import jax
import jax.numpy as jnp
from jax import lax
from jax.sharding import Mesh, PartitionSpec as P

AXES = ("z", "h", "x", "l", "k")
SIZES = {"z": 8, "h": 2, "x": 4, "l": 2, "k": 2}


def shift(value, axis, step):
    size = SIZES[axis]
    return lax.ppermute(value, axis, [(i, (i + step) % size) for i in range(size)])


def after(values, others):
    return lax.optimization_barrier((tuple(values), tuple(others)))[0]


def far_of(below, above):
    half = below.shape[0] // 2
    return [shift(below[:half], "x", 1), shift(above[half:], "x", -1)]


def local(amplitudes, integrals, ab_symmetry, cd_symmetry, ij_symmetry):
    rows = amplitudes.shape[0]
    width = integrals.shape[1]
    at = {name: lax.axis_index(name) for name in AXES}
    l, k = at["l"], at["k"]

    def columns(l, k):
        return lax.dynamic_slice_in_dim(amplitudes, (l * 2 + k) * width, width, axis=1)

    def chip_columns(l):
        return jnp.concatenate([columns(l, k), columns(l, 1 - k)], axis=1)

    give = chip_columns(1 - l)
    far = shift(give, "l", 1)
    mine = chip_columns(l)
    slabs = jnp.concatenate([mine, far], axis=0)

    up, down = [slabs], [slabs]
    for _ in range(3):
        up.append(shift(up[-1], "z", 1))
        down.append(shift(down[-1], "z", -1))
    opposite = [shift(up[-1][:rows], "z", 1), shift(down[-1][rows:], "z", -1)]
    opposite = lax.optimization_barrier(opposite)
    lines = jnp.zeros((8, 2 * rows, 2 * width), amplitudes.dtype)
    blocks = [slabs, up[1], down[1], up[2], down[2], up[3], down[3], jnp.concatenate(opposite, axis=0)]
    start = l * 2 * width
    cd_labels = [lax.dynamic_slice_in_dim(cd_symmetry, start + i * width, width) for i in (k, 1 - k)]
    cd_labels = jnp.concatenate(cd_labels)
    labels = lax.dynamic_index_in_dim(ij_symmetry.reshape(8, 8, rows), at["h"] * 4 + at["x"], 1, keepdims=False)
    labels = jnp.concatenate([labels, shift(labels, "l", 1)], axis=1)
    for step, block in zip((0, -1, 1, -2, 2, -3, 3, 4), blocks):
        label = lax.dynamic_index_in_dim(labels, (at["z"] + step) % 8, 0, keepdims=False)
        block = jnp.where(label[:, None] == cd_labels[None, :], block, jnp.zeros_like(block))
        lines = lax.dynamic_update_index_in_dim(lines, block, (at["z"] + step) % 8, 0)
    lines = lines.reshape(16 * rows, 2 * width)

    masked = integrals
    (block,) = after((masked,), (give,))
    below, above = shift(block, "x", 1), shift(block, "x", -1)
    (block,) = after((masked,), (far,))
    other = shift(block, "h", 1)
    middle = jnp.concatenate(far_of(below, above), axis=0)
    near = jnp.concatenate([masked, below, middle, above], axis=0)
    middle = shift(middle, "h", 1)
    below, above = shift(other, "x", 1), shift(other, "x", -1)
    sides = jnp.concatenate([other, below, above], axis=0)
    near_there = shift(near, "k", 1)
    sides_there = shift(sides, "k", 1)
    middle_there = shift(middle, "k", 1)

    def product(lines, here, there):
        both = (here, lines[:, :width]), (there, lines[:, width:])
        parts = [
            lax.dot_general(line, block, (((1,), (1,)), ((), ())), preferred_element_type=jnp.float32)
            for block, line in both
        ]
        return (parts[0] + parts[1]).reshape(8, 2, rows, 4 * 128)

    def in_order(sides, middle):
        return jnp.concatenate([sides[:256], middle, sides[256:]], axis=0)

    other = product(lines, in_order(sides, middle), in_order(sides_there, middle_there))

    def packed(summed):
        give = summed.reshape(-1, summed.shape[-1])
        step = jnp.maximum(jnp.max(jnp.abs(give), axis=0, keepdims=True), 1e-30) * (1 / 32512.0)
        power = jnp.ceil(jnp.log2(step) * 128.0)
        give = jnp.round(give * jnp.exp2(power * (-1 / 128.0))).astype(jnp.int16)
        power = jnp.broadcast_to(power, (8, power.shape[1])).astype(jnp.int16)
        return jnp.concatenate([give, power], axis=0)

    def unpacked(got):
        n = got.shape[0] - 8
        got = got.astype(jnp.float32)
        return got[:n] * jnp.exp2(got[n : n + 1] * (1 / 128.0))

    to_h, to_hl = packed(other[:, 0]), packed(other[:, 1])
    near = product(after((lines,), (to_hl,))[0], near, near_there)
    got_l = shift(packed(near[:, 1]), "l", 1)
    got_h = shift(to_h, "h", 1)
    got_hl = lax.ppermute(to_hl, ("h", "l"), [(0, 3), (1, 2), (2, 1), (3, 0)])
    own = near[:, 0].reshape(-1, 4 * 128) + unpacked(got_l)
    other = unpacked(got_h) + unpacked(got_hl)
    result = jnp.stack([own, other]).astype(jnp.bfloat16)
    home = [result[:, :, :128]]
    home += [shift(result[:, :, dx * 128 : dx * 128 + 128], "x", -dx) for dx in (1, 2, 3)]

    out = jnp.stack(home).reshape(4, 2, 8, rows, 128)
    out = out.transpose(2, 1, 0, 3, 4)
    out = jnp.roll(out, (at["h"], at["x"],), axis=(1, 2,)).reshape(64 * rows, 128)
    keep = ij_symmetry[:, None] == ab_symmetry[None, :]
    return jnp.where(keep, out, jnp.zeros_like(out))


def solution(mesh):
    fine = Mesh(mesh.devices.reshape(tuple(SIZES.values())), AXES)
    ab, cd = ("z", "h", "x"), ("l", "k")
    placed = (P(cd + ab, None), P(ab, cd), P(ab), P(), P(cd))
    return jax.shard_map(
        local, mesh=fine, in_specs=placed, out_specs=P(cd, ab), check_vma=False
    )
```

```python
import jax
import jax.numpy as jnp
from jax import lax
from jax.sharding import Mesh, PartitionSpec as P

AXES = ("z", "h", "x", "l", "k")
SIZES = {"z": 8, "h": 2, "x": 4, "l": 2, "k": 2}


def shift(value, axis, step):
    size = SIZES[axis]
    return lax.ppermute(value, axis, [(i, (i + step) % size) for i in range(size)])


def after(values, others):
    return lax.optimization_barrier((tuple(values), tuple(others)))[0]


def far_of(below, above):
    half = below.shape[0] // 2
    return [shift(below[:half], "x", 1), shift(above[half:], "x", -1)]


def local(amplitudes, integrals, ab_symmetry, cd_symmetry, ij_symmetry):
    rows = amplitudes.shape[0]
    width = integrals.shape[1]
    at = {name: lax.axis_index(name) for name in AXES}
    l, k = at["l"], at["k"]

    def columns(l, k):
        return lax.dynamic_slice_in_dim(amplitudes, (l * 2 + k) * width, width, axis=1)

    def chip_columns(l):
        return jnp.concatenate([columns(l, k), columns(l, 1 - k)], axis=1)

    give = chip_columns(1 - l)
    far = shift(give, "l", 1)
    mine = chip_columns(l)
    slabs = jnp.concatenate([mine, far], axis=0)

    up, down = [slabs], [slabs]
    for _ in range(3):
        up.append(shift(up[-1], "z", 1))
        down.append(shift(down[-1], "z", -1))
    opposite = [shift(up[-1][:rows], "z", 1), shift(down[-1][rows:], "z", -1)]
    lines = jnp.zeros((8, 2 * rows, 2 * width), amplitudes.dtype)
    blocks = [slabs, up[1], down[1], up[2], down[2], up[3], down[3]]
    start = l * 2 * width
    cd_labels = [lax.dynamic_slice_in_dim(cd_symmetry, start + i * width, width) for i in (k, 1 - k)]
    cd_labels = jnp.concatenate(cd_labels)
    labels = lax.dynamic_index_in_dim(ij_symmetry.reshape(8, 8, rows), at["h"] * 4 + at["x"], 1, keepdims=False)
    labels = jnp.concatenate([labels, shift(labels, "l", 1)], axis=1)
    def place(lines, step, block, first):
        label = lax.dynamic_index_in_dim(labels, (at["z"] + step) % 8, 0, keepdims=False)
        label = label[first : first + block.shape[0]]
        block = jnp.where(label[:, None] == cd_labels[None, :], block, jnp.zeros_like(block))
        return lax.dynamic_update_slice(lines, block[None], ((at["z"] + step) % 8, first, 0))

    for step, block in zip((0, -1, 1, -2, 2, -3, 3), blocks):
        lines = place(lines, step, block, 0)
    lines = place(place(lines, 4, opposite[0], 0), 4, opposite[1], rows)
    lines = lines.reshape(16 * rows, 2 * width)

    masked = integrals
    (block,) = after((masked,), (give,))
    below, above = shift(block, "x", 1), shift(block, "x", -1)
    (block,) = after((masked,), (far,))
    other = shift(block, "h", 1)
    middle = jnp.concatenate(far_of(below, above), axis=0)
    near = jnp.concatenate([masked, below, middle, above], axis=0)
    middle = shift(middle, "h", 1)
    below, above = shift(other, "x", 1), shift(other, "x", -1)
    sides = jnp.concatenate([other, below, above], axis=0)
    near_there = shift(near, "k", 1)
    sides_there = shift(sides, "k", 1)
    middle_there = shift(middle, "k", 1)

    def product(lines, here, there):
        both = (here, lines[:, :width]), (there, lines[:, width:])
        parts = [
            lax.dot_general(line, block, (((1,), (1,)), ((), ())), preferred_element_type=jnp.float32)
            for block, line in both
        ]
        return (parts[0] + parts[1]).reshape(8, 2, rows, 4 * 128)

    def in_order(sides, middle):
        return jnp.concatenate([sides[:256], middle, sides[256:]], axis=0)

    other = product(lines, in_order(sides, middle), in_order(sides_there, middle_there))

    def packed(summed):
        give = summed.reshape(-1, summed.shape[-1])
        step = jnp.maximum(jnp.max(jnp.abs(give), axis=0, keepdims=True), 1e-30) * (1 / 32512.0)
        power = jnp.ceil(jnp.log2(step) * 128.0)
        give = jnp.round(give * jnp.exp2(power * (-1 / 128.0))).astype(jnp.int16)
        power = jnp.broadcast_to(power, (8, power.shape[1])).astype(jnp.int16)
        return jnp.concatenate([give, power], axis=0)

    def unpacked(got):
        n = got.shape[0] - 8
        got = got.astype(jnp.float32)
        return got[:n] * jnp.exp2(got[n : n + 1] * (1 / 128.0))

    to_h, to_hl = packed(other[:, 0]), packed(other[:, 1])
    near = product(after((lines,), (to_hl,))[0], near, near_there)
    got_l = shift(packed(near[:, 1]), "l", 1)
    got_h = shift(to_h, "h", 1)
    got_hl = lax.ppermute(to_hl, ("h", "l"), [(0, 3), (1, 2), (2, 1), (3, 0)])
    own = near[:, 0].reshape(-1, 4 * 128) + unpacked(got_l)
    other = unpacked(got_h) + unpacked(got_hl)
    result = jnp.stack([own, other]).astype(jnp.bfloat16)
    home = [result[:, :, :128]]
    home += [shift(result[:, :, dx * 128 : dx * 128 + 128], "x", -dx) for dx in (1, 2, 3)]

    out = jnp.stack(home).reshape(4, 2, 8, rows, 128)
    out = out.transpose(2, 1, 0, 3, 4)
    out = jnp.roll(out, (at["h"], at["x"],), axis=(1, 2,)).reshape(64 * rows, 128)
    keep = ij_symmetry[:, None] == ab_symmetry[None, :]
    return jnp.where(keep, out, jnp.zeros_like(out))


def solution(mesh):
    fine = Mesh(mesh.devices.reshape(tuple(SIZES.values())), AXES)
    ab, cd = ("z", "h", "x"), ("l", "k")
    placed = (P(cd + ab, None), P(ab, cd), P(ab), P(), P(cd))
    return jax.shard_map(
        local, mesh=fine, in_specs=placed, out_specs=P(cd, ab), check_vma=False
    )
```
